128 devices in a mesh: dp: 32 (over x, y, core), fsdp: 4 (over z).
Axes of the slice: x: 4, y: 4, z: 4, core: 2. Of those that a mesh axis runs over, the one named last changes fastest.
Arguments:
- tokens: bfloat16 [65536, 4608], P(('dp', 'fsdp')), as said below
- rmsnorm_gain_vector: bfloat16 [4608], replicated, may hold values from 0.099609375 to 1.8984375
- tied_query_matrix: bfloat16 [4608, 2048], P('fsdp'), may hold values from -0.09375 to 0.09375
- adapter_down_matrix: bfloat16 [4608, 128], P('fsdp'), may hold values from -0.09375 to 0.09375
- adapter_up_matrix: bfloat16 [128, 2048], replicated, may hold values from -0.5 to 0.5
- depth: int32 [4096], P(('dp', 'fsdp')), may hold values from 1 to 3, as said below
- destination: int32 [4096], P(('dp', 'fsdp')), may hold values from 0 to 31, as said below
- cotangent: bfloat16 [32768, 2048], P(('dp', 'fsdp')), may hold values from -6 to 6
Outputs:
- query: bfloat16 [32768, 2048], P(('dp', 'fsdp'))
- grad_tokens: bfloat16 [65536, 4608], P(('dp', 'fsdp'))
- grad_down: float32 [4608, 128], replicated
- grad_up: float32 [128, 2048], replicated
The draws below stay inside these ranges and needn't reach their ends.
Inputs may be any that keep to these rules, and one draw needn't show every extreme that they name: Blocks that stop before this recursion have depth 1; the others have depth 2 or 3. `destination`: only entries of surviving blocks are read. Each dp index is named by exactly 16 surviving blocks with its own fsdp index, and by at most 1 surviving blocks of any one device; both bounds are reached in every draw. `tokens`: float values of mixed row and feature scales.
All inputs are finite; a program needn't handle non-finite values.
Results may differ from the reference program's by a relative error of at most 0.0053.
Values may be sent and summed in bfloat16 or wider, within the bound.
No kernel may reach another device: no remote copies, remote signals or barrier semaphores. Data moves between devices by JAX's collectives and lax.ppermute only.
A program may use at most 128 MiB of HBM per device.

```python
import jax
import jax.numpy as jnp
from jax import lax

MODEL_WIDTH = 4608
QUERY_FEATURES = 2048
ADAPTER_RANK = 128
BLK = 16
BLK_DEV = 32
CAP = 16
TOKENS = 65536
NBLK = 4096
OUT_ROWS = 32768
N_DP = 32
N_FSDP = 4


def block_plan(key):
    keys = jax.random.split(key, 6)
    pair_perm = jax.vmap(lambda k: jax.random.permutation(k, N_DP))(jax.random.split(keys[0], N_FSDP))
    halves = jax.random.randint(keys[1], (N_FSDP, N_DP // 2), 0, BLK_DEV + 1)
    halves = halves.at[:, 0].set(BLK_DEV)
    by_place = jnp.stack([halves, BLK_DEV - halves], axis=-1).reshape(N_FSDP, N_DP).astype(jnp.int32)
    counts = jax.vmap(lambda p, c: jnp.zeros((N_DP,), jnp.int32).at[p].set(c))(pair_perm, by_place)
    ranks = jax.vmap(lambda k: jax.random.permutation(k, BLK_DEV))(jax.random.split(keys[2], N_FSDP * N_DP))
    ranks = ranks.reshape(N_FSDP, N_DP, BLK_DEV)
    live = ranks < counts[:, :, None]
    flat = live.reshape(N_FSDP, N_DP * BLK_DEV).astype(jnp.int32)
    counter = jnp.cumsum(flat, axis=1) - flat
    recv_perm = jax.vmap(lambda k: jax.random.permutation(k, N_DP))(jax.random.split(keys[3], N_FSDP))
    receiver = jnp.take_along_axis(recv_perm, counter % N_DP, axis=1).reshape(N_FSDP, N_DP, BLK_DEV)
    deep = jax.random.randint(keys[4], (N_FSDP, N_DP, BLK_DEV), 2, 4)
    stray = jax.random.randint(keys[5], (N_FSDP, N_DP, BLK_DEV), 0, N_DP)
    depth = jnp.where(live, deep, 1)
    target = jnp.where(live, receiver, stray)
    depth = jnp.transpose(depth, (1, 0, 2)).reshape(-1).astype(jnp.int32)
    target = jnp.transpose(target, (1, 0, 2)).reshape(-1).astype(jnp.int32)
    return (depth, target)


def draw_depth(key, part):
    depth, target = block_plan(key)
    return depth


def draw_destination(key, part):
    depth, target = block_plan(key)
    return target


def draw_tokens(key, part):
    key = jax.random.fold_in(key, 11)
    keys = jax.random.split(key, 3)
    row_scale = jnp.exp(jax.random.uniform(keys[1], (TOKENS, 1), jnp.float32) * jnp.log(10.0))
    col_scale = jnp.exp(jax.random.uniform(keys[2], (1, MODEL_WIDTH), jnp.float32) * jnp.log(10.0))
    shared_output = jax.random.normal(keys[0], (TOKENS, MODEL_WIDTH), jnp.float32)
    return (shared_output * row_scale * col_scale).astype(jnp.bfloat16)


def block_scale(own_key, extent, cuts, least, top_value):
    def one(dim, blocks):
        draws = jax.random.uniform(jax.random.fold_in(jax.random.fold_in(own_key, 6), dim), (blocks,), jnp.float32, least / len(cuts), top_value / len(cuts))
        return jnp.repeat(jnp.exp(draws), extent[dim] // blocks).reshape((-1,) + (1,) * (len(extent) - dim - 1))

    factor_of = one(*cuts[0])
    for cut in cuts[1:]:
        factor_of = factor_of * one(*cut)
    return factor_of


def scatter_about(own_key, shape, scale, most, cuts=(), kind=jnp.bfloat16):
    result = scale * jax.random.normal(own_key, shape, jnp.float32)
    if cuts:
        result = result * block_scale(own_key, shape, cuts, -0.22, 0.18)
    return jnp.clip(result, -most, most).astype(kind)


def setup_inputs(seed: int = 0) -> dict:
    arg_keys = jax.random.split(jax.random.key(seed), 9)
    tokens = draw_tokens(jax.random.fold_in(arg_keys[8], 71), 0)
    rmsnorm_gain_vector = jnp.clip(1.0 + 0.18 * jax.random.normal(arg_keys[1], (MODEL_WIDTH,), jnp.float32), 0.099609375, 1.8984375).astype(jnp.bfloat16)
    tied_query_matrix = scatter_about(arg_keys[2], (MODEL_WIDTH, QUERY_FEATURES), MODEL_WIDTH ** -0.5, 0.09375, ((0, 4),))
    adapter_down_matrix = scatter_about(arg_keys[3], (MODEL_WIDTH, ADAPTER_RANK), MODEL_WIDTH ** -0.5, 0.09375, ((0, 4),))
    adapter_up_matrix = scatter_about(arg_keys[4], (ADAPTER_RANK, QUERY_FEATURES), ADAPTER_RANK ** -0.5, 0.5)
    depth = draw_depth(jax.random.fold_in(arg_keys[8], 71), 0)
    destination = draw_destination(jax.random.fold_in(arg_keys[8], 71), 0)
    cotangent = scatter_about(arg_keys[7], (OUT_ROWS, QUERY_FEATURES), 1.0, 6.0, ((0, 128),))
    return dict(tokens=tokens, rmsnorm_gain_vector=rmsnorm_gain_vector, tied_query_matrix=tied_query_matrix, adapter_down_matrix=adapter_down_matrix, adapter_up_matrix=adapter_up_matrix, depth=depth, destination=destination, cotangent=cotangent)


def reference(tokens, rmsnorm_gain_vector, tied_query_matrix, adapter_down_matrix, adapter_up_matrix, depth, destination, cotangent):
    devices = N_DP * N_FSDP
    live = depth >= 2
    order = jnp.arange(NBLK, dtype=jnp.int32)
    column = order // BLK_DEV % N_FSDP
    owner = (destination * N_FSDP + column).astype(jnp.int32)

    def count_step(counts, item):
        owner_now, live_now = item
        position = counts[owner_now]
        counts = counts.at[owner_now].add(live_now.astype(jnp.int32))
        return (counts, position)
    _, position = lax.scan(count_step, jnp.zeros((devices,), jnp.int32), (owner, live))
    target = (owner * CAP + position).astype(jnp.int32)
    live_index = jnp.nonzero(live, size=CAP * devices)[0].astype(jnp.int32)
    target_live = target[live_index]
    input_rows = tokens.reshape(NBLK, BLK, MODEL_WIDTH)[live_index].reshape(-1, MODEL_WIDTH)
    incoming_gradient_rows = cotangent.reshape(CAP * devices, BLK, QUERY_FEATURES)[target_live].reshape(-1, QUERY_FEATURES)
    xfloat = input_rows.astype(jnp.float32)
    inverse = lax.rsqrt(lax.optimization_barrier(jnp.mean(xfloat * xfloat, axis=-1, keepdims=True)) + 1e-06)
    normed = xfloat * inverse
    gain_f = rmsnorm_gain_vector.astype(jnp.float32)
    normalized_blocks = (normed * gain_f).astype(jnp.bfloat16)
    lowrank_hidden = jnp.dot(normalized_blocks, adapter_down_matrix, preferred_element_type=jnp.float32).astype(jnp.bfloat16)
    shared_output = jnp.dot(normalized_blocks, tied_query_matrix, preferred_element_type=jnp.float32)
    projected_query_rows = (shared_output + jnp.dot(lowrank_hidden, adapter_up_matrix, preferred_element_type=jnp.float32)).astype(jnp.bfloat16)
    grad_up = jnp.dot(lowrank_hidden.T, incoming_gradient_rows, preferred_element_type=jnp.float32)
    gradient_lowrank = jnp.dot(incoming_gradient_rows, adapter_up_matrix.T, preferred_element_type=jnp.float32).astype(jnp.bfloat16)
    grad_down = jnp.dot(normalized_blocks.T, gradient_lowrank, preferred_element_type=jnp.float32)
    gradient_normalized = jnp.dot(incoming_gradient_rows, tied_query_matrix.T, preferred_element_type=jnp.float32)
    gradient_normalized = gradient_normalized + jnp.dot(gradient_lowrank, adapter_down_matrix.T, preferred_element_type=jnp.float32)
    dscaled = gradient_normalized * gain_f
    grad_rows = inverse * (dscaled - normed * lax.optimization_barrier(jnp.mean(dscaled * normed, axis=-1, keepdims=True)))
    query = jnp.zeros((CAP * devices, BLK, QUERY_FEATURES), jnp.bfloat16)
    query = query.at[target_live].set(projected_query_rows.reshape(-1, BLK, QUERY_FEATURES)).reshape(-1, QUERY_FEATURES)
    grad_tokens = jnp.zeros((NBLK, BLK, MODEL_WIDTH), jnp.bfloat16)
    grad_tokens = grad_tokens.at[live_index].set(grad_rows.astype(jnp.bfloat16).reshape(-1, BLK, MODEL_WIDTH))
    return (query, grad_tokens.reshape(TOKENS, MODEL_WIDTH), grad_down, grad_up)
```

```python
import jax
import jax.numpy as jnp
from jax import lax
from jax.sharding import Mesh, PartitionSpec as P

DP = ("x", "y", "core")
BF16 = jnp.bfloat16
F32 = jnp.float32


def dot(a, b, dims=((1,), (0,))):
    return lax.dot_general(a, b, (dims, ((), ())), preferred_element_type=F32)


def gather_down(down):
    me = lax.axis_index("fsdp")
    rows = down.shape[0]
    full = jnp.zeros((4 * rows, down.shape[1]), down.dtype)
    for step in range(4):
        part = down
        if step:
            part = lax.ppermute(down, "fsdp", [((i + step) % 4, i) for i in range(4)])
        full = lax.dynamic_update_slice(full, part, (((me + step) % 4) * rows, 0))
    return full


def gather_weight(weight):
    chip = lax.axis_index("x") * 4 + lax.axis_index("y")
    half = weight.shape[1] // 2
    rows = weight.shape[0] // 16
    piece = lax.dynamic_slice(weight, (chip * rows, lax.axis_index("core") * half), (rows, half))
    both = lax.all_gather(piece, ("core", "fsdp", "x", "y"), axis=0, tiled=True)
    return both.reshape(2, both.shape[0] // 2, half)


def reduce_gradients(grads):
    rows, lanes = grads.shape
    parts = lax.all_to_all(grads.astype(BF16), DP, 0, 0, tiled=True)
    mine = jnp.sum(parts.reshape(32, rows // 32, lanes).astype(F32), axis=0)
    mine = lax.psum(mine, "fsdp")
    return lax.all_gather(mine, DP, axis=0, tiled=True)


def body(tokens, gain, weight, down, up, depth, destination, cotangent):
    blocks = depth.shape[0]
    rows, width = tokens.shape
    block_rows = rows // blocks
    features = cotangent.shape[1]
    capacity = cotangent.shape[0] // block_rows
    live = depth >= 2
    dest = jnp.clip(destination, 0, 31)

    hit = live[None, :] & (dest[None, :] == jnp.arange(32, dtype=jnp.int32)[:, None])
    order = jnp.arange(blocks, dtype=jnp.int32)
    source = jnp.sum(jnp.where(hit, order[None, :], 0), axis=1)
    sent = jnp.any(hit, axis=1).astype(jnp.int32)
    flags = lax.all_to_all(sent, DP, 0, 0, tiled=True)
    rank = jnp.sum(jnp.where(order[None, :] < order[:, None], flags[None, :], 0), axis=1)
    seat = jnp.clip(rank, 0, capacity - 1)
    seats = jnp.arange(capacity, dtype=jnp.int32)
    match = (flags[None, :] > 0) & (rank[None, :] == seats[:, None])
    pick = jnp.sum(jnp.where(match, order[None, :], 0), axis=1)

    full_weight = gather_weight(weight)
    full_down = gather_down(down)

    g_send = jnp.take(cotangent.reshape(capacity, block_rows, features), seat, axis=0)
    g_got = lax.all_to_all(g_send, DP, 0, 0, tiled=True)
    g = jnp.where(live[:, None, None], jnp.take(g_got, dest, axis=0), jnp.zeros((), BF16))
    g = g.reshape(rows, features)

    x = tokens.astype(F32)
    inverse = lax.rsqrt(jnp.mean(x * x, axis=-1, keepdims=True) + 1e-06)
    gain_f = gain.astype(F32)
    xn = (x * inverse * gain_f).astype(BF16)
    low = dot(xn, full_down).astype(BF16)
    dlow = dot(g, up, ((1,), (1,))).astype(BF16)
    grad_up = dot(low, g, ((0,), (0,)))
    grad_down = dot(xn, dlow, ((0,), (0,)))
    grads = jnp.concatenate([grad_down, grad_up.reshape(-1, grad_down.shape[1])], axis=0)
    grads = reduce_gradients(grads)
    grad_down, grad_up = grads[:width], grads[width:].reshape(grad_up.shape)

    half = features // 2
    q = jnp.concatenate([dot(xn, full_weight[0]), dot(xn, full_weight[1])], axis=1)
    q = (q + dot(low, up)).astype(BF16).reshape(blocks, block_rows, features)
    q_got = lax.all_to_all(jnp.take(q, source, axis=0), DP, 0, 0, tiled=True)
    query = jnp.take(q_got, pick, axis=0).reshape(capacity * block_rows, features)

    dxn = dot(g[:, :half], full_weight[0], ((1,), (1,))) + dot(g[:, half:], full_weight[1], ((1,), (1,)))
    dxn = dxn + dot(dlow, full_down, ((1,), (1,)))
    dy = dxn * gain_f
    normed = x * inverse
    grad_tokens = inverse * (dy - normed * jnp.mean(dy * normed, axis=-1, keepdims=True))
    grad_tokens = jnp.where(jnp.repeat(live, block_rows)[:, None], grad_tokens, 0.0).astype(BF16)
    return query, grad_tokens, grad_down, grad_up


def solution(mesh):
    fine = Mesh(mesh.devices.reshape(4, 4, 2, 4), ("x", "y", "core", "fsdp"))
    split = P(("x", "y", "core", "fsdp"))
    in_specs = (split, P(), P("fsdp"), P("fsdp"), P(), split, split, split)
    return jax.shard_map(
        body, mesh=fine, in_specs=in_specs, out_specs=(split, split, P(), P()), check_vma=False
    )
```

```python
import functools

import jax
import jax.numpy as jnp
from jax import lax
from jax.experimental import pallas as pl
from jax.experimental.pallas import tpu as pltpu
from jax.sharding import Mesh, PartitionSpec as P

DP = ("x", "y", "core")
BF16 = jnp.bfloat16
F32 = jnp.float32
CHUNKS = 2
MIB = 1024 * 1024


def dot(a, b, dims=((1,), (0,))):
    return lax.dot_general(a, b, (dims, ((), ())), preferred_element_type=F32)


def fetch(v, axis, step):
    n = lax.axis_size(axis)
    return lax.ppermute(v, axis, [((i + step) % n, i) for i in range(n)])


def gather_down(down):
    me = lax.axis_index("fsdp")
    rows = down.shape[0]
    full = jnp.zeros((4 * rows, down.shape[1]), down.dtype)
    for step in range(4):
        part = fetch(down, "fsdp", step) if step else down
        full = lax.dynamic_update_slice(full, part, (((me + step) % 4) * rows, 0))
    return full


def far_cut(rows):
    return (rows // 2 + 127) // 128 * 128


def gather_chunk(weight, chunk):
    rows = weight.shape[0]
    cols = weight.shape[1] // CHUNKS
    half = cols // 2
    mine = lax.dynamic_slice(
        weight, (0, chunk * cols + lax.axis_index("core") * half), (rows, half)
    )
    after = fetch(mine, "fsdp", 1)
    before = fetch(mine, "fsdp", 3)
    cut = far_cut(rows)
    far_top = fetch(after[:cut], "fsdp", 1)
    far_low = fetch(before[cut:], "fsdp", 3)
    own = [after, before, far_top, far_low]
    return own + [fetch(p, "core", 1) for p in own]


def sum_scatter(v, axis, wire):
    n = lax.axis_size(axis)
    me = lax.axis_index(axis)
    m = v.shape[0] // n
    total = lax.dynamic_slice_in_dim(v, me * m, m, 0)
    for step in range(1, n):
        part = lax.dynamic_slice_in_dim(v, ((me + n - step) % n) * m, m, 0).astype(wire)
        total = total + fetch(part, axis, step).astype(F32)
    return total


def sum_all(v, axis):
    n = lax.axis_size(axis)
    me = lax.axis_index(axis)
    parts = jnp.zeros((n,) + v.shape, v.dtype)
    for step in range(n):
        part = fetch(v, axis, step) if step else v
        parts = lax.dynamic_update_slice(parts, part[None], ((me + step) % n, 0, 0))
    return jnp.sum(parts, axis=0)


def collect(v, axis):
    n = lax.axis_size(axis)
    me = lax.axis_index(axis)
    m = v.shape[0]
    full = jnp.zeros((n * m, v.shape[1]), v.dtype)
    for step in range(n):
        part = fetch(v, axis, step) if step else v
        full = lax.dynamic_update_slice(full, part, (((me + step) % n) * m, 0))
    return full


def reduce_gradients(grads):
    v = sum_scatter(grads, "core", F32)
    v = sum_scatter(v, "fsdp", BF16)
    v = sum_scatter(v, "x", F32)
    v = sum_all(v, "y").astype(BF16)
    for axis in ("x", "fsdp", "core"):
        v = collect(v, axis)
    return v.astype(F32)


def piece_list(rows):
    cut = far_cut(rows)
    return [(1, 0, rows), (3, 0, rows), (2, 0, cut), (2, cut, rows - cut)]


def forward_kernel(chunk, where, source, xn, low, up, own, *refs):
    pieces, out = refs[:8], refs[8]
    held, own_held, q, sems = refs[9:17], refs[17], refs[18], refs[19]
    me, core = where[0], where[1]
    rows = own.shape[0]
    cols = own_held.shape[1]
    half = cols // 2
    copies = [pltpu.make_async_copy(own.at[:, pl.ds(chunk * cols, cols)], own_held, sems.at[8])]
    copies += [pltpu.make_async_copy(p, h, sems.at[i]) for i, (p, h) in enumerate(zip(pieces, held))]
    for c in copies:
        c.start()
    copies[0].wait()
    for side in range(2):
        at = pl.multiple_of((core if side == 0 else 1 - core) * half, half)
        acc = dot(low[...], up[:, pl.ds(at, half)])
        acc = acc + dot(xn[:, pl.ds(pl.multiple_of(me * rows, 128), rows)], own_held[:, pl.ds(at, half)])
        for i, (shard, first, size) in enumerate(piece_list(rows)):
            copies[1 + side * 4 + i].wait()
            at_row = pl.multiple_of(lax.rem(me + shard, 4) * rows + first, 128)
            acc = acc + dot(xn[:, pl.ds(at_row, size)], held[side * 4 + i][...])
        q[:, pl.ds(at, half)] = acc.astype(BF16)

    def place(d, carry):
        row = pl.multiple_of(source[d] * 16, 16)
        out[pl.ds(pl.multiple_of(d * 16, 16), 16), :] = q[pl.ds(row, 16), :]
        return carry

    lax.fori_loop(0, out.shape[0] // 16, place, 0)


def vmem():
    return pl.BlockSpec(memory_space=pltpu.VMEM)


def smem():
    return pl.BlockSpec(memory_space=pltpu.SMEM)


def anywhere():
    return pl.BlockSpec(memory_space=pl.ANY)


def forward(chunk, where, source, xn, low, up, own, pieces):
    tokens = xn.shape[0]
    cols = own.shape[1] // CHUNKS
    up = up[:, chunk * cols : (chunk + 1) * cols]
    return pl.pallas_call(
        functools.partial(forward_kernel, chunk),
        out_shape=jax.ShapeDtypeStruct((tokens, cols), BF16),
        in_specs=[smem(), smem(), vmem(), vmem(), vmem()] + [anywhere()] * 9,
        out_specs=vmem(),
        scratch_shapes=[pltpu.VMEM(p.shape, BF16) for p in pieces]
        + [
            pltpu.VMEM((own.shape[0], cols), BF16),
            pltpu.VMEM((tokens, cols), BF16),
            pltpu.SemaphoreType.DMA((9,)),
        ],
        compiler_params=pltpu.CompilerParams(vmem_limit_bytes=40 * MIB),
        cost_estimate=pl.CostEstimate(
            flops=2 * tokens * xn.shape[1] * cols, bytes_accessed=16 * MIB, transcendentals=0
        ),
        name="forward",
    )(where, source, xn, low, up, own, *pieces)


def backward_kernel(where, g, dlow, down, x, inverse, gain, live, own, *refs):
    count = 8 * CHUNKS
    pieces, out = refs[:count], refs[count]
    held, own_held, dxn, sems = refs[count + 1 : 2 * count + 1], *refs[2 * count + 1 :]
    me, core = where[0], where[1]
    rows = own.shape[0]
    cols = own.shape[1] // CHUNKS
    half = cols // 2
    copies = [pltpu.make_async_copy(own, own_held, sems.at[count])]
    copies += [pltpu.make_async_copy(p, h, sems.at[i]) for i, (p, h) in enumerate(zip(pieces, held))]
    for c in copies:
        c.start()
    nt = ((1,), (1,))
    tall = g.shape[0]
    base = pl.multiple_of(me * rows, 128)
    copies[0].wait()
    dxn[:, pl.ds(base, rows)] = dot(dlow[...], down[pl.ds(base, rows), :], nt) + dot(g[...], own_held[...], nt)
    for i, (shard, first, size) in enumerate(piece_list(rows)):
        base = pl.multiple_of(lax.rem(me + shard, 4) * rows + first, 128)
        acc = dot(dlow[...], down[pl.ds(base, size), :], nt)
        for chunk in range(CHUNKS):
            for side in range(2):
                n = chunk * 8 + side * 4 + i
                copies[1 + n].wait()
                at = pl.multiple_of(chunk * cols + (core if side == 0 else 1 - core) * half, half)
                acc = acc + dot(g[:, pl.ds(at, half)], held[n][...], nt)
        dxn[:, pl.ds(base, size)] = acc

    def finish(i, carry):
        r = pl.ds(pl.multiple_of(i * 16, 16), 16)
        inv = inverse[r, :]
        dy = dxn[r, :] * gain[...]
        normed = x[r, :].astype(F32) * inv
        mean = jnp.mean(dy * normed, axis=-1, keepdims=True)
        res = jnp.where(live[i] > 0, inv * (dy - normed * mean), 0.0)
        out[r, :] = res.astype(BF16)
        return carry

    lax.fori_loop(0, tall // 16, finish, 0)


def backward(where, g, dlow, down, x, inverse, gain, live, own, pieces):
    tokens, width = x.shape
    return pl.pallas_call(
        backward_kernel,
        out_shape=jax.ShapeDtypeStruct((tokens, width), BF16),
        in_specs=[smem()] + [vmem()] * 6 + [smem()] + [anywhere()] * (1 + len(pieces)),
        out_specs=vmem(),
        scratch_shapes=[pltpu.VMEM(p.shape, BF16) for p in pieces]
        + [
            pltpu.VMEM(own.shape, BF16),
            pltpu.VMEM((tokens, width), F32),
            pltpu.SemaphoreType.DMA((len(pieces) + 1,)),
        ],
        compiler_params=pltpu.CompilerParams(vmem_limit_bytes=56 * MIB),
        cost_estimate=pl.CostEstimate(
            flops=2 * tokens * width * own.shape[1], bytes_accessed=32 * MIB, transcendentals=0
        ),
        name="backward",
    )(where, g, dlow, down, x, inverse, gain, live, own, *pieces)


def body(tokens, gain, weight, down, up, depth, destination, cotangent):
    blocks = depth.shape[0]
    rows, width = tokens.shape
    block_rows = rows // blocks
    features = cotangent.shape[1]
    capacity = cotangent.shape[0] // block_rows
    cols = features // CHUNKS
    live = depth >= 2
    dest = jnp.clip(destination, 0, 31)
    where = jnp.stack([lax.axis_index("fsdp"), lax.axis_index("core")]).astype(jnp.int32)

    hit = live[None, :] & (dest[None, :] == jnp.arange(32, dtype=jnp.int32)[:, None])
    order = jnp.arange(blocks, dtype=jnp.int32)
    source = jnp.sum(jnp.where(hit, order[None, :], 0), axis=1)
    sent = jnp.any(hit, axis=1).astype(jnp.int32)
    flags = lax.all_to_all(sent, DP, 0, 0, tiled=True)
    rank = jnp.sum(jnp.where(order[None, :] < order[:, None], flags[None, :], 0), axis=1)
    seat = jnp.clip(rank, 0, capacity - 1)
    seats = jnp.arange(capacity, dtype=jnp.int32)
    match = (flags[None, :] > 0) & (rank[None, :] == seats[:, None])
    pick = jnp.sum(jnp.where(match, order[None, :], 0), axis=1)

    full_down = gather_down(down)
    pieces = [gather_chunk(weight, chunk) for chunk in range(CHUNKS)]

    g_send = jnp.take(cotangent.reshape(capacity, block_rows, features), seat, axis=0)
    g_got = lax.all_to_all(g_send, DP, 0, 0, tiled=True)
    g = jnp.where(live[:, None, None], jnp.take(g_got, dest, axis=0), jnp.zeros((), BF16))
    g = g.reshape(rows, features)

    x = tokens.astype(F32)
    inverse = lax.rsqrt(jnp.mean(x * x, axis=-1, keepdims=True) + 1e-06)
    gain_f = gain.astype(F32)
    xn = (x * inverse * gain_f).astype(BF16)
    low = dot(xn, full_down).astype(BF16)
    dlow = dot(g, up, ((1,), (1,))).astype(BF16)
    grad_up = dot(low, g, ((0,), (0,)))
    grad_down = dot(xn, dlow, ((0,), (0,)))
    grads = jnp.concatenate([grad_down, grad_up.reshape(-1, grad_down.shape[1])], axis=0)
    grads = reduce_gradients(grads)
    grad_down, grad_up = grads[:width], grads[width:].reshape(grad_up.shape)

    got = []
    for chunk in range(CHUNKS):
        q = forward(chunk, where, source, xn, low, up, weight, pieces[chunk])
        q = lax.all_to_all(q.reshape(blocks, block_rows, cols), DP, 0, 0, tiled=True)
        got.append(jnp.take(q, pick, axis=0).reshape(capacity * block_rows, cols))
    query = jnp.concatenate(got, axis=1)

    grad_tokens = backward(
        where, g, dlow, full_down, tokens, inverse, gain_f.reshape(1, width),
        live.astype(jnp.int32), weight, [p for c in pieces for p in c],
    )
    return query, grad_tokens, grad_down, grad_up


def solution(mesh):
    fine = Mesh(mesh.devices.reshape(4, 4, 2, 4), ("x", "y", "core", "fsdp"))
    split = P(("x", "y", "core", "fsdp"))
    in_specs = (split, P(), P("fsdp"), P("fsdp"), P(), split, split, split)
    return jax.shard_map(
        body, mesh=fine, in_specs=in_specs, out_specs=(split, split, P(), P()), check_vma=False
    )
```

```python
import jax
import jax.numpy as jnp
from jax import lax
from jax.experimental import pallas as pl
from jax.experimental.pallas import tpu as pltpu
from jax.sharding import Mesh, PartitionSpec as P

DP = ("x", "y", "core")
BF16 = jnp.bfloat16
F32 = jnp.float32
CHUNKS = 2
MIB = 1024 * 1024


def dot(a, b, dims=((1,), (0,))):
    return lax.dot_general(a, b, (dims, ((), ())), preferred_element_type=F32)


def fetch(v, axis, step):
    n = lax.axis_size(axis)
    return lax.ppermute(v, axis, [((i + step) % n, i) for i in range(n)])


def gather_down(down):
    me = lax.axis_index("fsdp")
    rows = down.shape[0]
    full = jnp.zeros((4 * rows, down.shape[1]), down.dtype)
    for step in range(4):
        part = fetch(down, "fsdp", step) if step else down
        full = lax.dynamic_update_slice(full, part, (((me + step) % 4) * rows, 0))
    return full


def gather_weight(weight):
    chip = lax.axis_index("x") * 4 + lax.axis_index("y")
    half = weight.shape[1] // 2
    rows = weight.shape[0] // 16
    piece = lax.dynamic_slice(weight, (chip * rows, lax.axis_index("core") * half), (rows, half))
    both = lax.all_gather(piece, ("core", "fsdp", "x", "y"), axis=0, tiled=True)
    return both.reshape(2, both.shape[0] // 2, half)


def sum_scatter(v, axis, wire):
    n = lax.axis_size(axis)
    me = lax.axis_index(axis)
    m = v.shape[0] // n
    total = lax.dynamic_slice_in_dim(v, me * m, m, 0)
    for step in range(1, n):
        part = lax.dynamic_slice_in_dim(v, ((me + n - step) % n) * m, m, 0).astype(wire)
        total = total + fetch(part, axis, step).astype(F32)
    return total


def sum_all(v, axis):
    n = lax.axis_size(axis)
    me = lax.axis_index(axis)
    parts = jnp.zeros((n,) + v.shape, v.dtype)
    for step in range(n):
        part = fetch(v, axis, step) if step else v
        parts = lax.dynamic_update_slice(parts, part[None], ((me + step) % n, 0, 0))
    return jnp.sum(parts, axis=0)


def collect(v, axis):
    n = lax.axis_size(axis)
    me = lax.axis_index(axis)
    m = v.shape[0]
    full = jnp.zeros((n * m, v.shape[1]), v.dtype)
    for step in range(n):
        part = fetch(v, axis, step) if step else v
        full = lax.dynamic_update_slice(full, part, (((me + step) % n) * m, 0))
    return full


def reduce_gradients(grads):
    v = sum_scatter(grads, "core", F32)
    v = sum_scatter(v, "fsdp", BF16)
    v = sum_scatter(v, "x", F32)
    v = sum_all(v, "y").astype(BF16)
    for axis in ("x", "fsdp", "core"):
        v = collect(v, axis)
    return v.astype(F32)


def forward_kernel(source, xn, low, w, up, out, q):
    q[...] = (dot(xn[...], w[0]) + dot(low[...], up[...])).astype(BF16)

    def place(d, carry):
        row = pl.multiple_of(source[d] * 16, 16)
        out[pl.ds(pl.multiple_of(d * 16, 16), 16), :] = q[pl.ds(row, 16), :]
        return carry

    lax.fori_loop(0, out.shape[0] // 16, place, 0)


def forward(chunk, source, xn, low, w, up):
    tokens, width = xn.shape
    cols = w.shape[2]
    tile = 512
    base = chunk * (cols // tile)
    return pl.pallas_call(
        forward_kernel,
        out_shape=jax.ShapeDtypeStruct((tokens, cols), BF16),
        grid_spec=pltpu.PrefetchScalarGridSpec(
            num_scalar_prefetch=1,
            grid=(cols // tile,),
            in_specs=[
                pl.BlockSpec((tokens, width), lambda i, s: (0, 0)),
                pl.BlockSpec(low.shape, lambda i, s: (0, 0)),
                pl.BlockSpec((1, width, tile), lambda i, s: (chunk, 0, i)),
                pl.BlockSpec((up.shape[0], tile), lambda i, s: (0, base + i)),
            ],
            out_specs=pl.BlockSpec((tokens, tile), lambda i, s: (0, i)),
            scratch_shapes=[pltpu.VMEM((tokens, tile), BF16)],
        ),
        compiler_params=pltpu.CompilerParams(vmem_limit_bytes=40 * MIB),
        cost_estimate=pl.CostEstimate(
            flops=2 * tokens * width * cols, bytes_accessed=16 * MIB, transcendentals=0
        ),
        name="forward",
    )(source, xn, low, w, up)


def backward_kernel(live, g, dlow, w, down, x, gain, inverse, out, dxn):
    i = pl.program_id(0)
    nt = ((1,), (1,))
    half = w.shape[2]
    tile = w.shape[1]
    acc = dot(g[:, :half], w[0], nt) + dot(g[:, half:], w[1], nt) + dot(dlow[...], down[...], nt)
    dxn[:, pl.ds(pl.multiple_of(i * tile, tile), tile)] = acc

    @pl.when(i == pl.num_programs(0) - 1)
    def _():
        def finish(j, carry):
            r = pl.ds(pl.multiple_of(j * 16, 16), 16)
            inv = inverse[r, :]
            dy = dxn[r, :] * gain[...]
            normed = x[r, :].astype(F32) * inv
            mean = jnp.mean(dy * normed, axis=-1, keepdims=True)
            res = jnp.where(live[j] > 0, inv * (dy - normed * mean), 0.0)
            out[r, :] = res.astype(BF16)
            return carry

        lax.fori_loop(0, x.shape[0] // 16, finish, 0)


def backward(live, g, dlow, w, down, x, gain, inverse):
    tokens, width = x.shape
    tile = 512

    def whole(v):
        return pl.BlockSpec(v.shape, lambda i, s: (0, 0))

    return pl.pallas_call(
        backward_kernel,
        out_shape=jax.ShapeDtypeStruct((tokens, width), BF16),
        grid_spec=pltpu.PrefetchScalarGridSpec(
            num_scalar_prefetch=1,
            grid=(width // tile,),
            in_specs=[
                whole(g),
                whole(dlow),
                pl.BlockSpec((2, tile, w.shape[2]), lambda i, s: (0, i, 0)),
                pl.BlockSpec((tile, down.shape[1]), lambda i, s: (i, 0)),
                whole(x),
                whole(gain),
                whole(inverse),
            ],
            out_specs=whole(x),
            scratch_shapes=[pltpu.VMEM((tokens, width), F32)],
        ),
        compiler_params=pltpu.CompilerParams(vmem_limit_bytes=56 * MIB),
        cost_estimate=pl.CostEstimate(
            flops=2 * tokens * width * g.shape[1], bytes_accessed=32 * MIB, transcendentals=0
        ),
        name="backward",
    )(live, g, dlow, w, down, x, gain, inverse)


def body(tokens, gain, weight, down, up, depth, destination, cotangent):
    blocks = depth.shape[0]
    rows, width = tokens.shape
    block_rows = rows // blocks
    features = cotangent.shape[1]
    capacity = cotangent.shape[0] // block_rows
    cols = features // CHUNKS
    live = depth >= 2
    dest = jnp.clip(destination, 0, 31)

    hit = live[None, :] & (dest[None, :] == jnp.arange(32, dtype=jnp.int32)[:, None])
    order = jnp.arange(blocks, dtype=jnp.int32)
    source = jnp.sum(jnp.where(hit, order[None, :], 0), axis=1)
    sent = jnp.any(hit, axis=1).astype(jnp.int32)
    flags = lax.all_to_all(sent, DP, 0, 0, tiled=True)
    rank = jnp.sum(jnp.where(order[None, :] < order[:, None], flags[None, :], 0), axis=1)
    seat = jnp.clip(rank, 0, capacity - 1)
    seats = jnp.arange(capacity, dtype=jnp.int32)
    match = (flags[None, :] > 0) & (rank[None, :] == seats[:, None])
    pick = jnp.sum(jnp.where(match, order[None, :], 0), axis=1)

    full_down = gather_down(down)
    full_weight = gather_weight(weight)

    g_send = jnp.take(cotangent.reshape(capacity, block_rows, features), seat, axis=0)
    g_got = lax.all_to_all(g_send, DP, 0, 0, tiled=True)
    g = jnp.where(live[:, None, None], jnp.take(g_got, dest, axis=0), jnp.zeros((), BF16))
    g = g.reshape(rows, features)

    x = tokens.astype(F32)
    inverse = lax.rsqrt(jnp.mean(x * x, axis=-1, keepdims=True) + 1e-06)
    gain_f = gain.astype(F32)
    xn = (x * inverse * gain_f).astype(BF16)
    low = dot(xn, full_down).astype(BF16)
    dlow = dot(g, up, ((1,), (1,))).astype(BF16)
    grad_up = dot(low, g, ((0,), (0,)))
    grad_down = dot(xn, dlow, ((0,), (0,)))
    grads = jnp.concatenate([grad_down, grad_up.reshape(-1, grad_down.shape[1])], axis=0)
    grads = reduce_gradients(grads)
    grad_down, grad_up = grads[:width], grads[width:].reshape(grad_up.shape)

    got = []
    for chunk in range(CHUNKS):
        q = forward(chunk, source, xn, low, full_weight, up)
        q = lax.all_to_all(q.reshape(blocks, block_rows, cols), DP, 0, 0, tiled=True)
        got.append(jnp.take(q, pick, axis=0).reshape(capacity * block_rows, cols))
    query = jnp.concatenate(got, axis=1)

    grad_tokens = backward(
        live.astype(jnp.int32), g, dlow, full_weight, full_down, tokens, gain_f.reshape(1, width), inverse
    )
    return query, grad_tokens, grad_down, grad_up


def solution(mesh):
    fine = Mesh(mesh.devices.reshape(4, 4, 2, 4), ("x", "y", "core", "fsdp"))
    split = P(("x", "y", "core", "fsdp"))
    in_specs = (split, P(), P("fsdp"), P("fsdp"), P(), split, split, split)
    return jax.shard_map(
        body, mesh=fine, in_specs=in_specs, out_specs=(split, split, P(), P()), check_vma=False
    )
```

```python
import jax
import jax.numpy as jnp
from jax import lax
from jax.experimental import pallas as pl
from jax.experimental.pallas import tpu as pltpu
from jax.sharding import Mesh, PartitionSpec as P

DP = ("x", "y", "core")
BF16 = jnp.bfloat16
F32 = jnp.float32
MIB = 1024 * 1024


def dot(a, b, dims=((1,), (0,))):
    return lax.dot_general(a, b, (dims, ((), ())), preferred_element_type=F32)


def fetch(v, axis, step):
    n = lax.axis_size(axis)
    return lax.ppermute(v, axis, [((i + step) % n, i) for i in range(n)])


def gather_down(down):
    me = lax.axis_index("fsdp")
    rows = down.shape[0]
    full = jnp.zeros((4 * rows, down.shape[1]), down.dtype)
    for step in range(4):
        part = fetch(down, "fsdp", step) if step else down
        full = lax.dynamic_update_slice(full, part, (((me + step) % 4) * rows, 0))
    return full


def gather_weight(weight):
    chip = lax.axis_index("x") * 4 + lax.axis_index("y")
    half = weight.shape[1] // 2
    rows = weight.shape[0] // 16
    piece = lax.dynamic_slice(weight, (chip * rows, lax.axis_index("core") * half), (rows, half))
    both = lax.all_gather(piece, ("core", "fsdp", "x", "y"), axis=0, tiled=True)
    return both.reshape(2, both.shape[0] // 2, half)


def sum_scatter(v, axis, wire):
    n = lax.axis_size(axis)
    me = lax.axis_index(axis)
    m = v.shape[0] // n
    total = lax.dynamic_slice_in_dim(v, me * m, m, 0)
    for step in range(1, n):
        part = lax.dynamic_slice_in_dim(v, ((me + n - step) % n) * m, m, 0).astype(wire)
        total = total + fetch(part, axis, step).astype(F32)
    return total


def sum_all(v, axis):
    n = lax.axis_size(axis)
    me = lax.axis_index(axis)
    parts = jnp.zeros((n,) + v.shape, v.dtype)
    for step in range(n):
        part = fetch(v, axis, step) if step else v
        parts = lax.dynamic_update_slice(parts, part[None], ((me + step) % n, 0, 0))
    return jnp.sum(parts, axis=0)


def tie(value, *others):
    return lax.optimization_barrier((value,) + others)[0]


def forward_kernel(source, xn, low, w, up, out, q):
    q[...] = (dot(xn[...], w[0]) + dot(low[...], up[...])).astype(BF16)

    def place(d, carry):
        row = pl.multiple_of(source[d] * 16, 16)
        out[pl.ds(pl.multiple_of(d * 16, 16), 16), :] = q[pl.ds(row, 16), :]
        return carry

    lax.fori_loop(0, out.shape[0] // 16, place, 0)


def forward(source, xn, low, w, up):
    tokens, width = xn.shape
    tile = 512
    per_half = w.shape[2] // tile
    cols = 2 * w.shape[2]
    return pl.pallas_call(
        forward_kernel,
        out_shape=jax.ShapeDtypeStruct((tokens, cols), BF16),
        grid_spec=pltpu.PrefetchScalarGridSpec(
            num_scalar_prefetch=1,
            grid=(cols // tile,),
            in_specs=[
                pl.BlockSpec((tokens, width), lambda i, s: (0, 0)),
                pl.BlockSpec(low.shape, lambda i, s: (0, 0)),
                pl.BlockSpec((1, width, tile), lambda i, s: (i // per_half, 0, i % per_half)),
                pl.BlockSpec((up.shape[0], tile), lambda i, s: (0, i)),
            ],
            out_specs=pl.BlockSpec((tokens, tile), lambda i, s: (0, i)),
            scratch_shapes=[pltpu.VMEM((tokens, tile), BF16)],
        ),
        compiler_params=pltpu.CompilerParams(vmem_limit_bytes=40 * MIB),
        cost_estimate=pl.CostEstimate(
            flops=2 * tokens * width * cols, bytes_accessed=26 * MIB, transcendentals=0
        ),
        name="forward",
    )(source, xn, low, w, up)


def backward_kernel(live, g, dlow, w, down, x, gain, inverse, out, held_dy, held_x, stat):
    i = pl.program_id(0)
    n = pl.num_programs(0)
    nt = ((1,), (1,))
    half = w.shape[2]
    tile = w.shape[1]
    inv = inverse[...]
    acc = dot(g[:, :half], w[0], nt) + dot(g[:, half:], w[1], nt) + dot(dlow[...], down[...], nt)
    dy = acc * gain[...]
    part = jnp.sum(dy * x[...].astype(F32), axis=-1, keepdims=True)
    stat[...] = part + jnp.where(i == 0, 0.0, stat[...])
    held_dy[i] = dy
    held_x[i] = x[...]

    @pl.when(i == n - 1)
    def _():
        factor = stat[...] * inv * inv * inv * (1.0 / (n * tile))
        stat[...] = factor

        def finish(j, carry):
            r = pl.ds(pl.multiple_of(j * 16, 16), 16)
            keep = live[j] > 0
            scale = inverse[r, :]
            shift = stat[r, :]
            for t in range(width_tiles(out, tile)):
                res = scale * held_dy[t, r, :] - shift * held_x[t, r, :].astype(F32)
                out[r, t * tile : (t + 1) * tile] = jnp.where(keep, res, 0.0).astype(BF16)
            return carry

        lax.fori_loop(0, out.shape[0] // 16, finish, 0)


def width_tiles(out, tile):
    return out.shape[1] // tile


def backward(live, g, dlow, w, down, x, gain, inverse):
    tokens, width = x.shape
    tile = 512
    n = width // tile
    cols = 2 * w.shape[2]
    return pl.pallas_call(
        backward_kernel,
        out_shape=jax.ShapeDtypeStruct((tokens, width), BF16),
        grid_spec=pltpu.PrefetchScalarGridSpec(
            num_scalar_prefetch=1,
            grid=(n,),
            in_specs=[
                pl.BlockSpec((tokens, cols), lambda i, s: (0, 0)),
                pl.BlockSpec(dlow.shape, lambda i, s: (0, 0)),
                pl.BlockSpec((2, tile, cols // 2), lambda i, s: (0, i, 0)),
                pl.BlockSpec((tile, down.shape[1]), lambda i, s: (i, 0)),
                pl.BlockSpec((tokens, tile), lambda i, s: (0, i)),
                pl.BlockSpec((1, tile), lambda i, s: (0, i)),
                pl.BlockSpec((tokens, 1), lambda i, s: (0, 0)),
            ],
            out_specs=pl.BlockSpec((tokens, width), lambda i, s: (0, 0)),
            scratch_shapes=[
                pltpu.VMEM((n, tokens, tile), F32),
                pltpu.VMEM((n, tokens, tile), BF16),
                pltpu.VMEM((tokens, 1), F32),
            ],
        ),
        compiler_params=pltpu.CompilerParams(vmem_limit_bytes=48 * MIB),
        cost_estimate=pl.CostEstimate(
            flops=2 * tokens * width * cols, bytes_accessed=32 * MIB, transcendentals=0
        ),
        name="backward",
    )(live, g, dlow, w, down, x, gain, inverse)


def body(tokens, gain, weight, down, up, depth, destination, cotangent):
    blocks = depth.shape[0]
    rows, width = tokens.shape
    block_rows = rows // blocks
    features = cotangent.shape[1]
    capacity = cotangent.shape[0] // block_rows
    live = depth >= 2
    dest = jnp.clip(destination, 0, 31)

    hit = live[None, :] & (dest[None, :] == jnp.arange(32, dtype=jnp.int32)[:, None])
    order = jnp.arange(blocks, dtype=jnp.int32)
    source = jnp.sum(jnp.where(hit, order[None, :], 0), axis=1)
    sent = jnp.any(hit, axis=1).astype(jnp.int32)
    flags = lax.all_to_all(sent, DP, 0, 0, tiled=True)
    rank = jnp.sum(jnp.where(order[None, :] < order[:, None], flags[None, :], 0), axis=1)
    seat = jnp.clip(rank, 0, capacity - 1)
    seats = jnp.arange(capacity, dtype=jnp.int32)
    match = (flags[None, :] > 0) & (rank[None, :] == seats[:, None])
    pick = jnp.sum(jnp.where(match, order[None, :], 0), axis=1)

    full_down = gather_down(down)
    x = tokens.astype(F32)
    inverse = lax.rsqrt(jnp.mean(x * x, axis=-1, keepdims=True) + 1e-06)
    weight, down = lax.optimization_barrier((weight, down, inverse))[:2]
    full_weight = gather_weight(weight)
    full_down = gather_down(down)
    gain_f = gain.astype(F32)
    xn = (x * inverse * gain_f).astype(BF16)
    low = dot(xn, full_down).astype(BF16)

    rank_width = low.shape[1]
    dlow_own = dot(cotangent, up, ((1,), (1,))).astype(BF16)
    narrow = jnp.concatenate(
        [
            jnp.take(low.reshape(blocks, block_rows, rank_width), source, axis=0),
            jnp.take(dlow_own.reshape(capacity, block_rows, rank_width), seat, axis=0),
        ],
        axis=2,
    )
    narrow = lax.all_to_all(narrow, DP, 0, 0, tiled=True)
    low_own = jnp.take(narrow[:, :, :rank_width], pick, axis=0).reshape(-1, rank_width)
    dlow = jnp.take(narrow[:, :, rank_width:], dest, axis=0)
    dlow = jnp.where(live[:, None, None], dlow, jnp.zeros((), BF16)).reshape(rows, rank_width)

    g_send = jnp.take(cotangent.reshape(capacity, block_rows, features), seat, axis=0)
    g_send = tie(g_send, narrow)
    g_got = lax.all_to_all(g_send, DP, 0, 0, tiled=True)
    g = jnp.where(live[:, None, None], jnp.take(g_got, dest, axis=0), jnp.zeros((), BF16))
    g = g.reshape(rows, features)

    grad_up = dot(low_own, cotangent, ((0,), (0,)))
    grad_down = dot(xn, dlow, ((0,), (0,)))
    lanes = features // rank_width
    grad_up = jnp.swapaxes(grad_up.reshape(rank_width, lanes, rank_width), 0, 1)
    grads = jnp.concatenate([grad_down, grad_up.reshape(features, rank_width)], axis=0)
    share = sum_scatter(grads, "core", F32)
    share = tie(sum_scatter(share, "fsdp", BF16), g_got)
    share = sum_scatter(share, "x", F32)
    share = sum_all(share, "y").astype(BF16)
    full_weight, share = lax.optimization_barrier((full_weight, share))
    grads = lax.all_gather(share, ("core", "fsdp", "x"), axis=0, tiled=True).astype(F32)
    grad_down = grads[:width]
    grad_up = jnp.swapaxes(grads[width:].reshape(lanes, rank_width, rank_width), 0, 1)
    grad_up = grad_up.reshape(rank_width, features)

    q = forward(source, xn, low, full_weight, up).reshape(blocks, block_rows, features)
    q = lax.all_to_all(q, DP, 0, 0, tiled=True)
    query = jnp.take(q, pick, axis=0).reshape(capacity * block_rows, features)

    grad_tokens = backward(
        live.astype(jnp.int32), g, dlow, full_weight, full_down, tokens, gain_f.reshape(1, width), inverse
    )
    return query, grad_tokens, grad_down, grad_up


def solution(mesh):
    fine = Mesh(mesh.devices.reshape(4, 4, 2, 4), ("x", "y", "core", "fsdp"))
    split = P(("x", "y", "core", "fsdp"))
    in_specs = (split, P(), P("fsdp"), P("fsdp"), P(), split, split, split)
    return jax.shard_map(
        body, mesh=fine, in_specs=in_specs, out_specs=(split, split, P(), P()), check_vma=False
    )
```
